32 devices in a mesh: grp: 2 (over y), col: 4 (over z), row: 4 (over x, core).
Axes of the slice: x: 2, y: 2, z: 4, core: 2. Of those that a mesh axis runs over, the one named last changes fastest.
Arguments:
- factor: float32 [8, 768, 3072], P(('grp', 'row'), 'col'), parts along dimension 0, may hold values from -1 to 3, as said below
- offsets: float32 [2, 16, 8192], P(None, None, ('grp', 'col')), parts along dimension 2, may hold values from -4 to 4
- targets_idx: int32 [16, 8192], P(None, ('grp', 'col')), parts along dimension 1, may hold values from 0 to 3071
- row_footprint: int32 [6144], P('grp'), parts along dimension 0, may hold values from 0 to 131071
- gain: float32 [243, 256], replicated, may hold values from 0.05 to 1
Outputs:
- weights: float32 [3072, 8192], P('row', ('grp', 'col')), parts along dimension 1
The draws below stay inside these ranges and needn't reach their ends.
There are 2 independent parts, one for each index of `grp`. The reference program is written for one: setup_inputs(seed, part) draws one part's arguments, and reference() takes and returns one part's arrays. A program takes and returns all parts, laid end to end along the dimension named above; an argument that names none is the same for every part. Nothing has to cross between parts.
Inputs may be any that keep to these rules, and one draw needn't show every extreme that they name: factor is lower triangular over the window's 3072 rows, with diagonal entries of 1 or more.
All inputs are finite; a program needn't handle non-finite values.
Results may differ from the reference program's by a relative error of at most 0.00022.
Values sent between devices are 32-bit elements; how exact they have to be, the bound alone decides.
A program may use at most 128 MiB of HBM per device.

```python
import math
import jax
import jax.numpy as jnp
from jax import lax

BS = 768
NT = 4096
K = 16
NPOS = 243
GRID = 16
PIX = 256
ORDER = 3072


def draw_factor(key, part):
    key = jax.random.fold_in(key, 11)
    key_off, key_main = jax.random.split(key)
    blocks = ORDER // BS
    shape = (blocks, BS, ORDER)
    global_row = lax.broadcasted_iota(jnp.int32, shape, 0) * BS + lax.broadcasted_iota(jnp.int32, shape, 1)
    global_col = lax.broadcasted_iota(jnp.int32, shape, 2)
    lower = jax.random.normal(key_off, shape, jnp.float32) * (0.45 / math.sqrt(ORDER))
    main = jax.random.uniform(key_main, shape, jnp.float32, 1.0, 2.0)
    return jnp.where(global_col < global_row, lower, jnp.where(global_col == global_row, main, 0.0))


def set_ends(array, stream_key, low, high):
    index_at = [jax.random.randint(jax.random.fold_in(stream_key, axis), (), 0, length) for axis, length in enumerate(array.shape)]
    widest = array.shape.index(max(array.shape))
    beside = index_at[:widest] + [(index_at[widest] + 1) % array.shape[widest]] + index_at[widest + 1:]
    return array.at[tuple(index_at)].set(low).at[tuple(beside)].set(high)


def shard_levels(rng, extent, cuts, low, top_value):
    level = 1.0
    for dim, parts in cuts:
        heights = jax.random.uniform(jax.random.fold_in(jax.random.fold_in(rng, 6), dim), (parts,), jnp.float32, low / len(cuts), top_value / len(cuts))
        level = level * jnp.repeat(jnp.exp(heights), extent[dim] // parts).reshape((-1,) + (1,) * (len(extent) - 1 - dim))
    return level


def setup_inputs(seed: int = 0, part: int = 0) -> dict:
    keys = jax.random.split(jax.random.key(seed), 6)
    part_keys = jax.random.split(jax.random.fold_in(keys[5], part), 6)
    return {
        "factor": draw_factor(jax.random.fold_in(jax.random.fold_in(keys[5], part), 71), part),
        "offsets": jnp.clip(jax.random.uniform(part_keys[1], (2, K, NT), jnp.float32, -4.0, 4.0) * shard_levels(part_keys[1], (2, K, NT), ((2, 4),), -0.4, 0.0), -4.0, 4.0),
        "targets_idx": set_ends(jax.random.randint(part_keys[2], (K, NT), 0, ORDER), jax.random.fold_in(part_keys[2], 1), 0, ORDER - 1).astype(jnp.int32),
        "row_footprint": set_ends(jax.random.randint(part_keys[3], (ORDER,), 0, 131072), jax.random.fold_in(part_keys[3], 1), 0, 131071).astype(jnp.int32),
        "gain": jnp.clip(jnp.exp(jax.random.uniform(keys[4], (NPOS, PIX), jnp.float32, math.log(0.05), math.log(1.0))), 0.05, 1.0),
    }


spread = 2.5

def responses(offsets):
    pixels = jnp.arange(GRID * GRID, dtype=jnp.int32)
    upos = (pixels // GRID).astype(jnp.float32) - (GRID - 1) / 2.0
    vpos = (pixels % GRID).astype(jnp.float32) - (GRID - 1) / 2.0
    delta_u = upos[None, None, :] - offsets[0][..., None]
    delta_v = vpos[None, None, :] - offsets[1][..., None]
    return jnp.exp(-(delta_u * delta_u + delta_v * delta_v) / (2.0 * spread * spread))

def reference(factor, offsets, targets_idx, row_footprint, gain):
    response = responses(offsets)
    positions = jnp.take(row_footprint, targets_idx) % NPOS
    patterns = gain[positions]
    correlation = jnp.sum(patterns * response, axis=-1) / jnp.sum(response, axis=-1)
    columns = jnp.broadcast_to(jnp.arange(NT, dtype=jnp.int32)[None, :], targets_idx.shape)
    rhs = jnp.zeros((ORDER, NT), jnp.float32).at[targets_idx, columns].add(correlation)
    lower_full = factor.reshape(ORDER, ORDER)
    solved = lax.linalg.triangular_solve(lower_full, rhs, left_side=True, lower=True)
    return lax.linalg.triangular_solve(lower_full, solved, left_side=True, lower=True, transpose_a=True)
```

```python
import functools

import jax
import jax.numpy as jnp
from jax import lax
from jax.experimental import pallas as pl
from jax.experimental.pallas import tpu as pltpu
from jax.sharding import PartitionSpec as P

NPOS = 243
GRID = 16
spread = 2.5
LANES = 128


def split(value):
    high = value.astype(jnp.bfloat16)
    return high, (value - high.astype(jnp.float32)).astype(jnp.bfloat16)


def dot3(left, right, contract):
    def one(a, b):
        return lax.dot_general(a, b, (contract, ((), ())), preferred_element_type=jnp.float32)

    return one(left[0], right[1]) + one(left[1], right[0]) + one(left[0], right[0])


def correlations(offsets, targets_idx, row_footprint, gain):
    members, count = targets_idx.shape
    pixels = jnp.arange(GRID * GRID, dtype=jnp.int32)
    upos = (pixels // GRID).astype(jnp.float32) - (GRID - 1) / 2.0
    vpos = (pixels % GRID).astype(jnp.float32) - (GRID - 1) / 2.0
    delta_u = upos[None, None, :] - offsets[0][..., None]
    delta_v = vpos[None, None, :] - offsets[1][..., None]
    response = jnp.exp(-(delta_u * delta_u + delta_v * delta_v) / (2.0 * spread * spread))
    table = (row_footprint % NPOS).astype(jnp.bfloat16).reshape(-1, LANES)
    upper = (targets_idx // LANES)[..., None] == jnp.arange(table.shape[0], dtype=jnp.int32)
    lower = (targets_idx % LANES)[..., None] == jnp.arange(LANES, dtype=jnp.int32)
    rows = jnp.einsum(
        "ktn,nl->ktl", upper.astype(jnp.bfloat16), table, preferred_element_type=jnp.float32
    )
    positions = jnp.sum(jnp.where(lower, rows, 0.0), axis=-1)
    chooser = (positions[..., None] == jnp.arange(NPOS, dtype=jnp.float32)).astype(jnp.bfloat16)
    first = lax.reduce_precision(gain, exponent_bits=8, mantissa_bits=7)
    second = lax.reduce_precision(gain - first, exponent_bits=8, mantissa_bits=7)
    parts = jnp.concatenate([first, second], axis=1).astype(jnp.bfloat16)
    both = jnp.einsum("ktn,np->ktp", chooser, parts, preferred_element_type=jnp.float32)
    patterns = both[..., : GRID * GRID] + both[..., GRID * GRID :]
    return jnp.sum(patterns * response, axis=-1) / jnp.sum(response, axis=-1)


def scatter(correlation, targets_idx, first_row, block_rows):
    local_rows = targets_idx - first_row
    row_iota = jnp.arange(block_rows, dtype=jnp.int32)[:, None]
    rhs = jnp.zeros((block_rows, targets_idx.shape[1]), jnp.float32)
    for member in range(targets_idx.shape[0]):
        rhs = rhs + jnp.where(
            row_iota == local_rows[member][None, :], correlation[member][None, :], 0.0
        )
    return rhs


class Plan:
    def __init__(self, rows, cols, part):
        self.rows, self.cols, self.part = rows, cols, part
        self.blocks = rows * cols
        self.half = part // 2
        self.chunks = [(j, h) for j in range(self.blocks) for h in range(2)]
        self.nodes = [(r, z) for r in range(rows) for z in range(cols)]
        self.parent = {c: self.tree(c) for c in self.chunks}
        self.simulate()

    def width(self, j):
        return -(-self.part * j // LANES) * LANES

    def slot(self):
        return -(-self.part // LANES) * LANES

    def tree(self, chunk):
        j, h = chunk
        r0, z0 = divmod(j, self.cols)
        both = r0 >= 2 and h == 1
        parent = {}
        for r, z in self.nodes:
            if (r, z) == (r0, z0):
                continue
            step = 1 if z < z0 else -1
            if r == r0:
                parent[r, z] = (r, z + step)
            elif r == r0 ^ 2:
                parent[r, z] = (r, z + step) if both and z != z0 else (r ^ 2, z)
            else:
                parent[r, z] = (r ^ 1, z)
        return parent

    def children(self, chunk, node):
        kids = [n for n, p in self.parent[chunk].items() if p == node]
        return sorted(kids, key=lambda n: (n[0] != node[0], n[0] ^ node[0] == 1, n))

    def simulate(self):
        free, self.arrival = {}, {}
        waiting = []
        for j, h in self.chunks:
            source = divmod(j, self.cols)
            self.arrival[(j, h), source] = 0.0
            waiting.append((0.0, j, h, source))
        while waiting:
            waiting.sort()
            when, j, h, node = waiting.pop(0)
            size = self.half * (self.width(j) + self.slot()) * 4
            for kid in self.children((j, h), node):
                if kid[0] ^ node[0] == 1:
                    link, rate = (node, kid), 300e3
                else:
                    link, rate = (node[0] // 2, node[1], kid[0] // 2, kid[1]), 90e3
                start = max(when, free.get(link, 0.0))
                free[link] = start + size / rate
                self.arrival[(j, h), kid] = free[link] + 1.0
                waiting.append((free[link] + 1.0, j, h, kid))

    def events(self, node):
        order = sorted(
            (c for c in self.chunks if divmod(c[0], self.cols) != node),
            key=lambda c: (self.arrival[c, node], c),
        )
        place = {c: i for i, c in enumerate(order)}
        lists, done = [], 0
        for j in range(self.blocks):
            need = max(place.get((j, h), -1) for h in range(2)) + 1
            lists.append(order[done:need])
            done = max(done, need)
        return lists


def kernel(plan, own_ref, rhs_ref, out_ref, factor, values, high, low, send, recv, local, back_send, back_recv):
    rank, place = lax.axis_index("row"), lax.axis_index("col")
    part, half, cols, blocks = plan.part, plan.half, plan.cols, plan.blocks
    count = values.shape[1]

    def at_node(action):
        for node in plan.nodes:
            pl.when(jnp.logical_and(rank == node[0], place == node[1]))(functools.partial(action, node))

    def target(node):
        return {"row": node[0], "col": node[1]}

    def chunk_copy(chunk, way, kid):
        j, h = chunk
        view = factor.at[j, pl.ds(h * half, half), pl.ds(0, plan.width(j) + plan.slot())]
        return pltpu.make_async_remote_copy(
            src_ref=view, dst_ref=view, send_sem=send.at[j * 2 + h, way], recv_sem=recv.at[j * 2 + h],
            device_id=target(kid), device_id_type=pl.DeviceIdType.MESH)

    def forward_chunk(chunk, node):
        for way, kid in enumerate(plan.children(chunk, node)):
            chunk_copy(chunk, way, kid).start()

    rhs_copy = pltpu.make_async_copy(rhs_ref, values, local.at[0])
    rhs_copy.start()
    barrier = pltpu.get_barrier_semaphore()

    def greet(node):
        r, z = node
        near = [(q, z) for q in range(plan.rows) if q != r]
        near += [(r, y) for y in (z - 1, z + 1) if 0 <= y < cols]
        for other in near:
            pl.semaphore_signal(barrier, inc=1, device_id=target(other), device_id_type=pl.DeviceIdType.MESH)
        pl.semaphore_wait(barrier, len(near))
        j = r * cols + z
        width = plan.width(j) + plan.slot()
        own = pltpu.make_async_copy(
            own_ref.at[:, pl.ds(0, width)], factor.at[j, :, pl.ds(0, width)], local.at[1])
        own.start()
        own.wait()
        for h in range(2):
            forward_chunk((j, h), node)

    at_node(greet)
    high[...] = jnp.zeros_like(high)
    low[...] = jnp.zeros_like(low)
    rhs_copy.wait()

    def take(j, node):
        for chunk in plan.events(node)[j]:
            kids = plan.children(chunk, node)
            chunk_copy(chunk, 0, kids[0] if kids else (node[0] ^ 1, node[1])).wait_recv()
            forward_chunk(chunk, node)

    def pieces(j, run):
        whole = 3 * LANES
        steps, rest = divmod(plan.width(j), whole)
        if steps:
            @pl.loop(0, steps)
            def _(step):
                run(pl.multiple_of(step * whole, whole), whole)
        if rest:
            run(steps * whole, rest)

    for j in range(blocks):
        at_node(functools.partial(take, j))
        rows = pl.ds(j * part, part)

        def ahead(start, size):
            left = split(factor[j, :, pl.ds(start, size)])
            right = high[pl.ds(start, size), :], low[pl.ds(start, size), :]
            values[rows, :] -= dot3(left, right, ((1,), (0,)))

        pieces(j, ahead)
        inverse = factor[j, :, pl.ds(plan.width(j), plan.slot())][:, :part]
        solved = dot3(split(inverse), split(values[rows, :]), ((1,), (0,)))
        values[rows, :] = solved
        high[rows, :], low[rows, :] = split(solved)

    def give(j, node, wait):
        r, z = node
        owner, inner = divmod(j, cols)
        source = values.at[pl.ds(j * part, part), :]
        goal = out_ref.at[pl.ds(inner * part, part), pl.ds(r * count, count)]
        if owner == r:
            copy = pltpu.make_async_copy(source, goal, back_send.at[j])
            copy.wait() if wait else copy.start()
            return
        copy = pltpu.make_async_remote_copy(
            src_ref=source, dst_ref=goal, send_sem=back_send.at[j], recv_sem=back_recv.at[inner, r],
            device_id=target((owner, z)), device_id_type=pl.DeviceIdType.MESH)
        copy.wait_send() if wait else copy.start()

    for j in reversed(range(blocks)):
        rows = pl.ds(j * part, part)
        inverse = factor[j, :, pl.ds(plan.width(j), plan.slot())]
        done = dot3(split(inverse), split(values[rows, :]), ((0,), (0,)))[:part]
        right = split(done)

        def behind(start, size):
            left = split(factor[j, :, pl.ds(start, size)])
            values[pl.ds(start, size), :] -= dot3(left, right, ((0,), (0,)))

        pieces(j, behind)
        values[rows, :] = done
        at_node(functools.partial(give, j, wait=False))

    def finish(node):
        r, z = node
        for j in range(blocks):
            give(j, node, True)
        for inner in range(cols):
            for other in range(plan.rows):
                if other == r:
                    continue
                source = values.at[pl.ds(0, part), :]
                goal = out_ref.at[pl.ds(inner * part, part), pl.ds(other * count, count)]
                pltpu.make_async_remote_copy(
                    src_ref=source, dst_ref=goal, send_sem=back_send.at[0],
                    recv_sem=back_recv.at[inner, other], device_id=target((other, z)),
                    device_id_type=pl.DeviceIdType.MESH).wait_recv()
        for chunk in plan.chunks:
            for way, kid in enumerate(plan.children(chunk, node)):
                chunk_copy(chunk, way, kid).wait_send()

    at_node(finish)


def fused(factor, offsets, targets_idx, row_footprint, gain):
    rank, place = lax.axis_index("row"), lax.axis_index("col")
    plan = Plan(lax.axis_size("row"), lax.axis_size("col"), factor.shape[1])
    part, order = factor.shape[1], factor.shape[2]
    count = targets_idx.shape[1] // plan.rows
    mine = factor[0]
    block = rank * plan.cols + place
    diagonal = lax.dynamic_slice_in_dim(mine, block * part, part, 1)
    inverse = lax.linalg.triangular_solve(
        diagonal, jnp.eye(part, dtype=jnp.float32), left_side=True, lower=True)
    inverse = jnp.pad(inverse, ((0, 0), (0, plan.slot() - part)))
    width = plan.width(plan.blocks - 1) + plan.slot()
    start = -(-(block * part) // LANES) * LANES
    own = lax.dynamic_update_slice(
        jnp.pad(mine, ((0, 0), (0, width - order))), inverse, (jnp.zeros_like(start), start))
    offsets = lax.dynamic_slice_in_dim(offsets, rank * count, count, 2)
    targets_idx = lax.dynamic_slice_in_dim(targets_idx, rank * count, count, 1)
    correlation = correlations(offsets, targets_idx, row_footprint, gain)
    rhs = scatter(correlation, targets_idx, 0, order)
    anywhere = pl.BlockSpec(memory_space=pl.ANY)
    return pl.pallas_call(
        functools.partial(kernel, plan),
        out_shape=jax.ShapeDtypeStruct((order // plan.rows, count * plan.rows), jnp.float32),
        in_specs=[anywhere, anywhere],
        out_specs=anywhere,
        scratch_shapes=[
            pltpu.VMEM((plan.blocks, part, width), jnp.float32),
            pltpu.VMEM((order, count), jnp.float32),
            pltpu.VMEM((order, count), jnp.bfloat16),
            pltpu.VMEM((order, count), jnp.bfloat16),
            pltpu.SemaphoreType.DMA((2 * plan.blocks, 4)),
            pltpu.SemaphoreType.DMA((2 * plan.blocks,)),
            pltpu.SemaphoreType.DMA((2,)),
            pltpu.SemaphoreType.DMA((plan.blocks,)),
            pltpu.SemaphoreType.DMA((plan.cols, plan.rows)),
        ],
        compiler_params=pltpu.CompilerParams(
            collective_id=0, has_side_effects=True, vmem_limit_bytes=60 * 1024 * 1024),
        cost_estimate=pl.CostEstimate(
            flops=2 * order * order * count, bytes_accessed=4 * order * order, transcendentals=0),
    )(own, rhs)


def product(left, right, contract):
    return lax.dot_general(
        left, right, (contract, ((), ())), precision=lax.Precision.HIGHEST,
        preferred_element_type=jnp.float32)


def stepped(factor, offsets, targets_idx, row_footprint, gain):
    row_rank = lax.axis_index("row")
    row_count = lax.axis_size("row")
    block_rows = factor.shape[2] // row_count

    def broadcast(value, source):
        return lax.psum(jnp.where(row_rank == source, value, 0.0), "row")

    row_panel = lax.all_gather(factor, "col", axis=1, tiled=True)[0]
    correlation = correlations(offsets, targets_idx, row_footprint, gain)
    rhs = scatter(correlation, targets_idx, row_rank * block_rows, block_rows)
    diagonal = lax.dynamic_slice_in_dim(row_panel, row_rank * block_rows, block_rows, 1)
    carried = jnp.zeros_like(rhs)
    solved_own = jnp.zeros_like(rhs)
    for step in range(row_count):
        candidate = lax.linalg.triangular_solve(diagonal, rhs - carried, left_side=True, lower=True)
        solved_own = jnp.where(row_rank == step, candidate, solved_own)
        if step + 1 < row_count:
            columns = row_panel[:, step * block_rows : (step + 1) * block_rows]
            carried = carried + product(columns, broadcast(candidate, step), ((1,), (0,)))
    weights_own = jnp.zeros_like(rhs)
    moved = lax.all_to_all(factor, "row", split_axis=2, concat_axis=0, tiled=True)
    column_panel = lax.all_gather(moved, "col", axis=1, tiled=True)
    carried = jnp.zeros_like(rhs)
    for step in reversed(range(row_count)):
        candidate = lax.linalg.triangular_solve(
            diagonal, solved_own - carried, left_side=True, lower=True, transpose_a=True)
        weights_own = jnp.where(row_rank == step, candidate, weights_own)
        if step > 0:
            carried = carried + product(column_panel[step], broadcast(candidate, step), ((0,), (0,)))
    return weights_own


def body(factor, offsets, targets_idx, row_footprint, gain):
    small = lax.axis_size("row") == 4 and factor.shape[1] % (3 * LANES // 2) == 0
    small = small and targets_idx.shape[1] % (4 * LANES) == 0
    run = fused if small else stepped
    return run(factor, offsets, targets_idx, row_footprint, gain)


def solution(mesh):
    in_specs = (
        P(("grp", "row"), "col", None),
        P(None, None, ("grp", "col")),
        P(None, ("grp", "col")),
        P("grp"),
        P(),
    )
    out_specs = P("row", ("grp", "col"))
    return jax.shard_map(body, mesh=mesh, in_specs=in_specs, out_specs=out_specs, check_vma=False)
```

```python
import functools

import jax
import jax.numpy as jnp
from jax import lax
from jax.experimental import pallas as pl
from jax.experimental.pallas import tpu as pltpu
from jax.sharding import PartitionSpec as P

NPOS = 243
GRID = 16
spread = 2.5
LANES = 128


def split(value):
    high = value.astype(jnp.bfloat16)
    return high, (value - high.astype(jnp.float32)).astype(jnp.bfloat16)


def dot3(left, right, contract):
    def one(a, b):
        return lax.dot_general(a, b, (contract, ((), ())), preferred_element_type=jnp.float32)

    return one(left[0], right[1]) + one(left[1], right[0]) + one(left[0], right[0])


def correlations(offsets, targets_idx, row_footprint, gain):
    members, count = targets_idx.shape
    pixels = jnp.arange(GRID * GRID, dtype=jnp.int32)
    upos = (pixels // GRID).astype(jnp.float32) - (GRID - 1) / 2.0
    vpos = (pixels % GRID).astype(jnp.float32) - (GRID - 1) / 2.0
    delta_u = upos[None, None, :] - offsets[0][..., None]
    delta_v = vpos[None, None, :] - offsets[1][..., None]
    response = jnp.exp(-(delta_u * delta_u + delta_v * delta_v) / (2.0 * spread * spread))
    table = (row_footprint % NPOS).astype(jnp.bfloat16).reshape(-1, LANES)
    upper = (targets_idx // LANES)[..., None] == jnp.arange(table.shape[0], dtype=jnp.int32)
    lower = (targets_idx % LANES)[..., None] == jnp.arange(LANES, dtype=jnp.int32)
    rows = jnp.einsum(
        "ktn,nl->ktl", upper.astype(jnp.bfloat16), table, preferred_element_type=jnp.float32
    )
    positions = jnp.sum(jnp.where(lower, rows, 0.0), axis=-1)
    chooser = (positions[..., None] == jnp.arange(NPOS, dtype=jnp.float32)).astype(jnp.bfloat16)
    first = lax.reduce_precision(gain, exponent_bits=8, mantissa_bits=7)
    second = lax.reduce_precision(gain - first, exponent_bits=8, mantissa_bits=7)
    parts = jnp.concatenate([first, second], axis=1).astype(jnp.bfloat16)
    both = jnp.einsum("ktn,np->ktp", chooser, parts, preferred_element_type=jnp.float32)
    patterns = both[..., : GRID * GRID] + both[..., GRID * GRID :]
    return jnp.sum(patterns * response, axis=-1) / jnp.sum(response, axis=-1)


def scatter(correlation, targets_idx, first_row, block_rows):
    local_rows = targets_idx - first_row
    row_iota = jnp.arange(block_rows, dtype=jnp.int32)[:, None]
    rhs = jnp.zeros((block_rows, targets_idx.shape[1]), jnp.float32)
    for member in range(targets_idx.shape[0]):
        rhs = rhs + jnp.where(
            row_iota == local_rows[member][None, :], correlation[member][None, :], 0.0
        )
    return rhs


class Plan:
    def __init__(self, rows, cols, part):
        self.rows, self.cols, self.part = rows, cols, part
        self.blocks = rows * cols
        self.half = part // 2
        self.chunks = [(j, h) for j in range(self.blocks) for h in range(3) if j or h == 2]
        self.nodes = [(r, z) for r in range(rows) for z in range(cols)]
        self.parent = {c: self.tree(c) for c in self.chunks}
        self.simulate()

    def width(self, j):
        return -(-self.part * j // LANES) * LANES

    def slot(self):
        return -(-self.part // LANES) * LANES

    def tree(self, chunk):
        j, h = chunk
        r0, z0 = divmod(j, self.cols)
        both = r0 >= 2 and h == 1
        parent = {}
        for r, z in self.nodes:
            if (r, z) == (r0, z0):
                continue
            step = 1 if z < z0 else -1
            if r == r0:
                parent[r, z] = (r, z + step)
            elif r == r0 ^ 2:
                parent[r, z] = (r, z + step) if both and z != z0 else (r ^ 2, z)
            else:
                parent[r, z] = (r ^ 1, z)
        return parent

    def children(self, chunk, node):
        kids = [n for n, p in self.parent[chunk].items() if p == node]
        return sorted(kids, key=lambda n: (n[0] != node[0], n[0] ^ node[0] == 1, n))

    def simulate(self):
        free, self.arrival = {}, {}
        waiting = []
        for j, h in self.chunks:
            source = divmod(j, self.cols)
            ready = 12.0 if h == 2 else 0.0
            self.arrival[(j, h), source] = ready
            waiting.append((ready, j, h, source))
        while waiting:
            waiting.sort()
            when, j, h, node = waiting.pop(0)
            size = (self.part * self.slot() if h == 2 else self.half * self.width(j)) * 4
            for kid in self.children((j, h), node):
                if kid[0] ^ node[0] == 1:
                    link, rate = (node, kid), 300e3
                else:
                    link, rate = (node[0] // 2, node[1], kid[0] // 2, kid[1]), 90e3
                start = max(when, free.get(link, 0.0))
                free[link] = start + size / rate
                self.arrival[(j, h), kid] = free[link] + 1.0
                waiting.append((free[link] + 1.0, j, h, kid))

    def events(self, node):
        order = sorted(
            (c for c in self.chunks if divmod(c[0], self.cols) != node),
            key=lambda c: (self.arrival[c, node], c),
        )
        place = {c: i for i, c in enumerate(order)}
        lists, done = [], 0
        for j in range(self.blocks):
            need = max(place.get((j, h), -1) for h in range(3)) + 1
            lists.append(order[done:need])
            done = max(done, need)
        return lists


def kernel(
    plan, own_ref, diagonal_ref, offsets_ref, targets_ref, table_ref, gain_ref, out_ref,
    factor, inverses, values, high, low, found, send, recv, local, back_send, back_recv,
):
    rank, place = lax.axis_index("row"), lax.axis_index("col")
    part, half, cols, blocks = plan.part, plan.half, plan.cols, plan.blocks
    count = values.shape[1]

    def at_node(action):
        for node in plan.nodes:
            pl.when(jnp.logical_and(rank == node[0], place == node[1]))(functools.partial(action, node))

    def target(node):
        return {"row": node[0], "col": node[1]}

    def chunk_copy(chunk, way, kid):
        j, h = chunk
        if h == 2:
            view = inverses.at[j]
        else:
            view = factor.at[j, pl.ds(h * half, half), pl.ds(0, plan.width(j))]
        return pltpu.make_async_remote_copy(
            src_ref=view, dst_ref=view, send_sem=send.at[j * 3 + h, way], recv_sem=recv.at[j * 3 + h],
            device_id=target(kid), device_id_type=pl.DeviceIdType.MESH)

    def forward_chunk(chunk, node):
        for way, kid in enumerate(plan.children(chunk, node)):
            chunk_copy(chunk, way, kid).start()

    barrier = pltpu.get_barrier_semaphore()

    def greet(node):
        r, z = node
        near = [(q, z) for q in range(plan.rows) if q != r]
        near += [(r, y) for y in (z - 1, z + 1) if 0 <= y < cols]
        for other in near:
            pl.semaphore_signal(barrier, inc=1, device_id=target(other), device_id_type=pl.DeviceIdType.MESH)
        j = r * cols + z
        width = plan.width(j)
        if j:
            own = pltpu.make_async_copy(
                own_ref.at[:, pl.ds(0, width)], factor.at[j, :, pl.ds(0, width)], local.at[0])
            own.start()
            own.wait()
        pl.semaphore_wait(barrier, len(near))
        if j:
            for h in range(2):
                forward_chunk((j, h), node)

    at_node(greet)

    diagonal = diagonal_ref[...]
    row = lax.broadcasted_iota(jnp.int32, (part, part), 0)
    column = lax.broadcasted_iota(jnp.int32, (part, part), 1)
    inverse = jnp.where(row == column, 1.0 / diagonal, 0.0)
    size = 1
    while size < part:
        pair = (row // (2 * size) == column // (2 * size)) & (row // size > column // size)
        off = jnp.where(pair, diagonal, 0.0)
        inverse = inverse - product(product(inverse, off, ((1,), (0,))), inverse, ((1,), (0,)))
        size *= 2

    block = rank * cols + place
    inverses[block, :, pl.ds(0, part)] = inverse
    if plan.slot() > part:
        inverses[block, :, pl.ds(part, plan.slot() - part)] = jnp.zeros(
            (part, plan.slot() - part), jnp.float32)
    at_node(lambda node: forward_chunk((node[0] * cols + node[1], 2), node))

    high[...] = jnp.zeros_like(high)
    low[...] = jnp.zeros_like(low)
    table = table_ref[...]
    gain_parts = split(gain_ref[...])
    along = lax.broadcasted_iota(jnp.int32, (GRID, count), 0).astype(jnp.float32) - (GRID - 1) / 2.0
    contract = ((1,), (0,))

    @pl.loop(0, targets_ref.shape[0])
    def _(member):
        rows = targets_ref[pl.ds(member, 1), :]
        upper = lax.broadcasted_iota(jnp.int32, (table.shape[1], count), 0) == rows // LANES
        lower = lax.broadcasted_iota(jnp.int32, (LANES, count), 0) == rows % LANES
        near = lax.dot_general(
            table, jnp.where(upper, 1.0, 0.0).astype(jnp.bfloat16), (contract, ((), ())),
            preferred_element_type=jnp.float32)
        position = jnp.sum(jnp.where(lower, near, 0.0), axis=0, keepdims=True).astype(jnp.int32)
        chosen = lax.broadcasted_iota(jnp.int32, (gain_ref.shape[1], count), 0) == position
        chooser = jnp.where(chosen, 1.0, 0.0).astype(jnp.bfloat16)
        pattern = sum(
            lax.dot_general(g, chooser, (contract, ((), ())), preferred_element_type=jnp.float32)
            for g in gain_parts)
        delta_u = along - offsets_ref[0, pl.ds(member, 1), :]
        delta_v = along - offsets_ref[1, pl.ds(member, 1), :]
        weight_u = jnp.exp(-(delta_u * delta_u) / (2.0 * spread * spread))
        weight_v = jnp.exp(-(delta_v * delta_v) / (2.0 * spread * spread))
        top = jnp.zeros((1, count), jnp.float32)
        for u in range(GRID):
            inner = jnp.sum(pattern[u * GRID : (u + 1) * GRID] * weight_v, axis=0, keepdims=True)
            top = top + weight_u[u : u + 1] * inner
        bottom = jnp.sum(weight_u, axis=0, keepdims=True) * jnp.sum(weight_v, axis=0, keepdims=True)
        found[pl.ds(member, 1), :] = top / bottom

    tall = 32

    @pl.loop(0, values.shape[0] // tall)
    def _(step):
        first = pl.multiple_of(step * tall, tall)
        iota = lax.broadcasted_iota(jnp.int32, (tall, count), 0) + first
        total = jnp.zeros((tall, count), jnp.float32)
        for member in range(targets_ref.shape[0]):
            here = iota == targets_ref[member : member + 1, :]
            total = total + jnp.where(here, found[member : member + 1, :], 0.0)
        values[pl.ds(first, tall), :] = total

    def take(j, node):
        for chunk in plan.events(node)[j]:
            kids = plan.children(chunk, node)
            chunk_copy(chunk, 0, kids[0] if kids else (node[0] ^ 1, node[1])).wait_recv()
            forward_chunk(chunk, node)

    def pieces(j, run):
        whole = 3 * LANES
        steps, rest = divmod(plan.width(j), whole)
        if steps:
            @pl.loop(0, steps)
            def _(step):
                run(pl.multiple_of(step * whole, whole), whole)
        if rest:
            run(steps * whole, rest)

    for j in range(blocks):
        at_node(functools.partial(take, j))
        rows = pl.ds(j * part, part)

        def ahead(start, size):
            left = split(factor[j, :, pl.ds(start, size)])
            right = high[pl.ds(start, size), :], low[pl.ds(start, size), :]
            values[rows, :] -= dot3(left, right, ((1,), (0,)))

        pieces(j, ahead)
        inverse = inverses[j][:, :part]
        solved = dot3(split(inverse), split(values[rows, :]), ((1,), (0,)))
        values[rows, :] = solved
        high[rows, :], low[rows, :] = split(solved)

    def give(j, node, wait):
        r, z = node
        owner, inner = divmod(j, cols)
        source = values.at[pl.ds(j * part, part), :]
        goal = out_ref.at[pl.ds(inner * part, part), pl.ds(r * count, count)]
        if owner == r:
            copy = pltpu.make_async_copy(source, goal, back_send.at[j])
            copy.wait() if wait else copy.start()
            return
        copy = pltpu.make_async_remote_copy(
            src_ref=source, dst_ref=goal, send_sem=back_send.at[j], recv_sem=back_recv.at[inner, r],
            device_id=target((owner, z)), device_id_type=pl.DeviceIdType.MESH)
        copy.wait_send() if wait else copy.start()

    for j in reversed(range(blocks)):
        rows = pl.ds(j * part, part)
        inverse = inverses[j]
        done = dot3(split(inverse), split(values[rows, :]), ((0,), (0,)))[:part]
        right = split(done)

        def behind(start, size):
            left = split(factor[j, :, pl.ds(start, size)])
            values[pl.ds(start, size), :] -= dot3(left, right, ((0,), (0,)))

        pieces(j, behind)
        values[rows, :] = done
        at_node(functools.partial(give, j, wait=False))

    def finish(node):
        r, z = node
        for j in range(blocks):
            give(j, node, True)
        for inner in range(cols):
            for other in range(plan.rows):
                if other == r:
                    continue
                source = values.at[pl.ds(0, part), :]
                goal = out_ref.at[pl.ds(inner * part, part), pl.ds(other * count, count)]
                pltpu.make_async_remote_copy(
                    src_ref=source, dst_ref=goal, send_sem=back_send.at[0],
                    recv_sem=back_recv.at[inner, other], device_id=target((other, z)),
                    device_id_type=pl.DeviceIdType.MESH).wait_recv()
        for chunk in plan.chunks:
            for way, kid in enumerate(plan.children(chunk, node)):
                chunk_copy(chunk, way, kid).wait_send()

    at_node(finish)


def fused(factor, offsets, targets_idx, row_footprint, gain):
    rank, place = lax.axis_index("row"), lax.axis_index("col")
    plan = Plan(lax.axis_size("row"), lax.axis_size("col"), factor.shape[1])
    part, order = factor.shape[1], factor.shape[2]
    count = targets_idx.shape[1] // plan.rows
    mine = factor[0]
    block = rank * plan.cols + place
    diagonal = lax.dynamic_slice_in_dim(mine, block * part, part, 1)
    width = plan.width(plan.blocks - 1)
    offsets = lax.dynamic_slice_in_dim(offsets, rank * count, count, 2)
    targets_idx = lax.dynamic_slice_in_dim(targets_idx, rank * count, count, 1)
    table = (row_footprint % NPOS).astype(jnp.bfloat16).reshape(-1, LANES).T
    table = jnp.pad(table, ((0, 0), (0, -table.shape[1] % LANES)))
    pattern = jnp.pad(gain.T, ((0, 0), (0, -NPOS % LANES)))
    inside = pl.BlockSpec(memory_space=pltpu.VMEM)
    anywhere = pl.BlockSpec(memory_space=pl.ANY)
    return pl.pallas_call(
        functools.partial(kernel, plan),
        out_shape=jax.ShapeDtypeStruct((order // plan.rows, count * plan.rows), jnp.float32),
        in_specs=[anywhere] + [inside] * 5,
        out_specs=anywhere,
        scratch_shapes=[
            pltpu.VMEM((plan.blocks, part, width), jnp.float32),
            pltpu.VMEM((plan.blocks, part, plan.slot()), jnp.float32),
            pltpu.VMEM((order, count), jnp.float32),
            pltpu.VMEM((order, count), jnp.bfloat16),
            pltpu.VMEM((order, count), jnp.bfloat16),
            pltpu.VMEM(targets_idx.shape, jnp.float32),
            pltpu.SemaphoreType.DMA((3 * plan.blocks, 4)),
            pltpu.SemaphoreType.DMA((3 * plan.blocks,)),
            pltpu.SemaphoreType.DMA((1,)),
            pltpu.SemaphoreType.DMA((plan.blocks,)),
            pltpu.SemaphoreType.DMA((plan.cols, plan.rows)),
        ],
        compiler_params=pltpu.CompilerParams(
            collective_id=0, has_side_effects=True, vmem_limit_bytes=60 * 1024 * 1024),
        cost_estimate=pl.CostEstimate(
            flops=2 * order * order * count, bytes_accessed=4 * order * order, transcendentals=0),
    )(mine, diagonal, offsets, targets_idx, table, pattern)


def product(left, right, contract):
    return lax.dot_general(
        left, right, (contract, ((), ())), precision=lax.Precision.HIGHEST,
        preferred_element_type=jnp.float32)


def stepped(factor, offsets, targets_idx, row_footprint, gain):
    row_rank = lax.axis_index("row")
    row_count = lax.axis_size("row")
    block_rows = factor.shape[2] // row_count

    def broadcast(value, source):
        return lax.psum(jnp.where(row_rank == source, value, 0.0), "row")

    row_panel = lax.all_gather(factor, "col", axis=1, tiled=True)[0]
    correlation = correlations(offsets, targets_idx, row_footprint, gain)
    rhs = scatter(correlation, targets_idx, row_rank * block_rows, block_rows)
    diagonal = lax.dynamic_slice_in_dim(row_panel, row_rank * block_rows, block_rows, 1)
    carried = jnp.zeros_like(rhs)
    solved_own = jnp.zeros_like(rhs)
    for step in range(row_count):
        candidate = lax.linalg.triangular_solve(diagonal, rhs - carried, left_side=True, lower=True)
        solved_own = jnp.where(row_rank == step, candidate, solved_own)
        if step + 1 < row_count:
            columns = row_panel[:, step * block_rows : (step + 1) * block_rows]
            carried = carried + product(columns, broadcast(candidate, step), ((1,), (0,)))
    weights_own = jnp.zeros_like(rhs)
    moved = lax.all_to_all(factor, "row", split_axis=2, concat_axis=0, tiled=True)
    column_panel = lax.all_gather(moved, "col", axis=1, tiled=True)
    carried = jnp.zeros_like(rhs)
    for step in reversed(range(row_count)):
        candidate = lax.linalg.triangular_solve(
            diagonal, solved_own - carried, left_side=True, lower=True, transpose_a=True)
        weights_own = jnp.where(row_rank == step, candidate, weights_own)
        if step > 0:
            carried = carried + product(column_panel[step], broadcast(candidate, step), ((0,), (0,)))
    return weights_own


def body(factor, offsets, targets_idx, row_footprint, gain):
    small = lax.axis_size("row") == 4 and factor.shape[1] % (3 * LANES // 2) == 0
    small = small and targets_idx.shape[1] % (4 * LANES) == 0
    run = fused if small else stepped
    return run(factor, offsets, targets_idx, row_footprint, gain)


def solution(mesh):
    in_specs = (
        P(("grp", "row"), "col", None),
        P(None, None, ("grp", "col")),
        P(None, ("grp", "col")),
        P("grp"),
        P(),
    )
    out_specs = P("row", ("grp", "col"))
    return jax.shard_map(body, mesh=mesh, in_specs=in_specs, out_specs=out_specs, check_vma=False)
```
